32 devices in a mesh: grp: 2 (over y), ra: 16 (over z, x, core).
Axes of the slice: x: 2, y: 2, z: 4, core: 2. Of those that a mesh axis runs over, the one named last changes fastest.
Arguments:
- split_maps: bfloat16 [4, 3, 1024, 2048], P(None, None, 'grp', 'ra'), parts along dimension 2, may hold values from -6 to 6
- tile_start: int32 [32, 2], P(('grp', 'ra')), parts along dimension 0, may hold values from 0 to 31, as said below
- pattern: int32 [32, 256], P('grp', 'ra'), parts along dimension 0, may hold values 0 or 1
Outputs:
- noise_model: float32 [32, 256, 6, 256], P('grp', 'ra'), parts along dimension 0
The draws below stay inside these ranges and needn't reach their ends.
There are 2 independent parts, one for each index of `grp`. The reference program is written for one: setup_inputs(seed, part) draws one part's arguments, and reference() takes and returns one part's arrays. A program takes and returns all parts, laid end to end along the dimension named above; each array names one. Nothing has to cross between parts.
Inputs may be any that keep to these rules, and one draw needn't show every extreme that they name: `tile_start`: tile t belongs to the device of index t // 1 along ra. Its first block row lies from 0 to 4. Its first block column, taken relative to 2 t (the first block column of its owner's strip) around the wrapping map, lies from -2 to 0; both ends are reached. A tile covers 4 by 4 blocks.
All inputs are finite; a program needn't handle non-finite values. No bound on the sum of `pattern` on one device may be relied on, other than what follows from the above.
Results may differ from the reference program's by a relative error of at most 0.0024.
Values may be sent and summed in bfloat16 or wider, within the bound.
A program may use at most 192 MiB of HBM per device.

```python
import math
import jax
import jax.numpy as jnp
from jax import lax

SPLITS = 4
STOKES = 3
BPX = 64
TB = 4
CBD = 2
REACH = 1
FBN = 16
RB = 8
TPD = 1
TILE = 256
FBS = 16
FBLK = 256
NT = 16
CB = 32
NROW = 512
NCOL = 2048


def draw_tile_start(key, part):
    key = jax.random.fold_in(key, 11)
    row_key, column_key = jax.random.split(key)
    counter = jnp.arange(NT, dtype=jnp.int32)
    owner = counter // TPD
    rows = jax.random.randint(row_key, (NT,), 0, RB - TB + 1, dtype=jnp.int32)
    rows = rows.at[0].set(0).at[NT - 1].set(RB - TB)
    lowest = -REACH * CBD
    highest = (REACH + 1) * CBD - TB
    middle = 1 - (TB + 1) // 2
    offset = jax.random.randint(column_key, (NT,), lowest, highest + 1, dtype=jnp.int32)
    offset = offset.at[0].set(middle).at[1].set(lowest).at[NT - 1].set(highest)
    columns = (owner * CBD + offset) % CB
    return jnp.stack([rows, columns], axis=1).astype(jnp.int32)


def plant(entries, key, smallest, high):
    longest = entries.shape.index(max(entries.shape))
    spots = []
    for shift in (0, 1):
        where = [jax.random.randint(jax.random.fold_in(key, axis), (), 0, length) for axis, length in enumerate(entries.shape)]
        where[longest] = (where[longest] + shift) % entries.shape[longest]
        spots.append(tuple(where))
    return entries.at[spots[0]].set(smallest).at[spots[1]].set(high)


def shard_levels(rng, extent, shards, smallest, top_value):
    factor_of, own = 1.0, jax.random.fold_in(rng, 6)
    for axis_at, shards_of in shards:
        draws = jnp.exp(jax.random.uniform(jax.random.fold_in(own, axis_at), (shards_of,), jnp.float32, smallest / len(shards), top_value / len(shards)))
        factor_of = factor_of * jnp.repeat(draws, extent[axis_at] // shards_of).reshape([-1 if axis == axis_at else 1 for axis in range(len(extent))])
    return factor_of


def centred(rng, extent, width, most, cuts=(), kind=jnp.bfloat16):
    result = jax.random.normal(rng, extent, jnp.float32) * width
    if len(cuts) > 0:
        result = shard_levels(rng, extent, cuts, -0.22, 0.18) * result
    return jnp.clip(result, min=-most, max=most).astype(kind)


def setup_inputs(seed: int = 0, part: int = 0) -> dict:
    splits = jax.random.split(jax.random.key(seed), 4)
    own_keys = jax.random.split(jax.random.fold_in(splits[3], part), 4)
    split_maps = centred(own_keys[0], (SPLITS, STOKES, NROW, NCOL), 1.0, 6.0, ((3, 16),))
    tile_start = draw_tile_start(jax.random.fold_in(jax.random.fold_in(splits[3], part), 71), part)
    pattern = plant((jax.random.randint(own_keys[2], (NT, FBLK), 0, 2) < 1).astype(jnp.int32), jax.random.fold_in(own_keys[2], 1), 0, 1)
    return {"split_maps": split_maps, "tile_start": tile_start, "pattern": pattern}


cov_pairs = ((0, 0), (1, 1), (2, 2), (0, 1), (0, 2), (1, 2))

def fourier_tables(length):
    counter = jnp.arange(length, dtype=jnp.int32)
    phase = counter[:, None] * counter[None, :] % length
    angle = 2.0 * math.pi / length * phase.astype(jnp.float32)
    factor = 1.0 / math.sqrt(length)
    return ((jnp.cos(angle) * factor).astype(jnp.bfloat16), (jnp.sin(angle) * factor).astype(jnp.bfloat16))

def taper_table(length):
    edge = length // 8
    counter = jnp.arange(length, dtype=jnp.float32)
    rising = jnp.where(counter < edge, jnp.sin(math.pi * (counter + 0.5) / (2 * edge)) ** 2, 1.0)
    line = rising * rising[::-1]
    return line[:, None] * line[None, :]

def blockify(spectra):
    count = spectra.shape[0]
    shaped = spectra.reshape(count, FBN, FBS, FBN, FBS)
    return shaped.transpose(1, 3, 0, 2, 4).reshape(FBN * FBN, count, FBS * FBS)

def cross_power(stacked):
    values = stacked.astype(jnp.float32)
    real_part = values[..., 0, :, :, :]
    imag_part = values[..., 1, :, :, :]
    terms = []
    for first_axis, second_axis in cov_pairs:
        product = real_part[..., first_axis, :] * real_part[..., second_axis, :] + imag_part[..., first_axis, :] * imag_part[..., second_axis, :]
        terms.append(lax.optimization_barrier(jnp.mean(product, axis=-2)))
    return jnp.stack(terms, axis=-2)

def tile_power(split_maps, corner, taper, section_one, section_two):
    row_start = (corner[0] * BPX).astype(jnp.int32)
    slab = lax.dynamic_slice_in_dim(split_maps, row_start, TILE, 2)
    columns = ((corner[1] * BPX + jnp.arange(TILE, dtype=jnp.int32)) % NCOL).astype(jnp.int32)
    pixels = jnp.take(slab, columns, axis=3).astype(jnp.float32)
    difference = pixels - lax.optimization_barrier(jnp.mean(pixels, axis=0, keepdims=True))
    tapered = (difference * taper).astype(jnp.bfloat16)
    flat = tapered.reshape(SPLITS * STOKES * TILE, TILE)
    halfway = jnp.dot(flat, section_one, preferred_element_type=jnp.float32).astype(jnp.bfloat16)
    halfway = halfway.reshape(SPLITS * STOKES, TILE, 2 * TILE)
    outer = jnp.einsum('ky,mya->mka', section_two.astype(jnp.float32), halfway.astype(jnp.float32), precision=lax.Precision.HIGHEST)
    real_part = outer[:, :TILE, :TILE] - outer[:, TILE:, TILE:]
    imag_part = outer[:, :TILE, TILE:] + outer[:, TILE:, :TILE]
    spectra = jnp.concatenate([real_part, imag_part], axis=0).astype(jnp.bfloat16)
    blocks = blockify(spectra)
    return cross_power(blocks.reshape(FBLK, 2, SPLITS, STOKES, FBS * FBS))

def reference(split_maps, tile_start, pattern):
    taper = taper_table(TILE)
    cosine, sine = fourier_tables(TILE)
    section_one = jnp.concatenate([cosine, sine], axis=1)
    section_two = jnp.concatenate([cosine, sine], axis=0)
    cross = lax.map(lambda corner: tile_power(split_maps, corner, taper, section_one, section_two), tile_start)
    block_mean = lax.optimization_barrier(jnp.mean(cross, axis=-1, keepdims=True))
    level = lax.optimization_barrier(jnp.mean(block_mean, axis=0, keepdims=True))
    kept = jnp.where((pattern == 1)[:, :, None, None], cross, block_mean)
    return 0.5 * kept + 0.5 * level
```

```python
import functools
import math

import jax
import jax.numpy as jnp
from jax import lax
from jax.experimental import pallas as pl
from jax.experimental.pallas import tpu as pltpu
from jax.sharding import PartitionSpec as P

SPLITS = 4
STOKES = 3
BPX = 64
CBD = 2
REACH = 1
FBN = 16
TILE = 256
FBS = 16
FBLK = 256
PAIRS = 6
COMBOS = 3
HALF = 128
MESH = pl.DeviceIdType.MESH


cov_pairs = ((0, 0), (1, 1), (2, 2), (0, 1), (0, 2), (1, 2))


def with_halo(shard, sides, width):
    for axis, dim in sides:
        size, length = (lax.axis_size(axis), shard.shape[dim])
        up = [(i, (i + 1) % size) for i in range(size)]
        down = [(j, i) for i, j in up]
        last = lax.slice_in_dim(shard, length - width, length, axis=dim)
        initial = lax.slice_in_dim(shard, 0, width, axis=dim)
        before = lax.ppermute(last, axis, up)
        after = lax.ppermute(initial, axis, down)
        shard = jnp.concatenate([before, shard, after], axis=dim)
    return shard


def fourier_tables(length):
    counter = jnp.arange(length, dtype=jnp.int32)
    phase = counter[:, None] * counter[None, :] % length
    angle = 2.0 * math.pi / length * phase.astype(jnp.float32)
    factor = 1.0 / math.sqrt(length)
    return (
        (jnp.cos(angle) * factor).astype(jnp.bfloat16),
        (jnp.sin(angle) * factor).astype(jnp.bfloat16),
    )


def taper_table(length):
    edge = length // 8
    counter = jnp.arange(length, dtype=jnp.float32)
    rising = jnp.where(counter < edge, jnp.sin(math.pi * (counter + 0.5) / (2 * edge)) ** 2, 1.0)
    line = rising * rising[::-1]
    return line[:, None] * line[None, :]


def blockify(spectra):
    count = spectra.shape[0]
    shaped = spectra.reshape(count, FBN, FBS, FBN, FBS)
    return shaped.transpose(1, 3, 0, 2, 4).reshape(FBN * FBN, count, FBS * FBS)


def cross_power(stacked):
    values = stacked.astype(jnp.float32)
    real_part = values[..., 0, :, :, :]
    imag_part = values[..., 1, :, :, :]
    terms = []
    for first_axis, second_axis in cov_pairs:
        product = (
            real_part[..., first_axis, :] * real_part[..., second_axis, :]
            + imag_part[..., first_axis, :] * imag_part[..., second_axis, :]
        )
        terms.append(jnp.mean(product, axis=-2))
    return jnp.stack(terms, axis=-2)


def plain_body(split_maps, tile_start, pattern):
    width = REACH * CBD * BPX
    window = with_halo(split_maps, (("ra", 3),), width)
    first_block = (lax.axis_index("ra") - REACH) * CBD
    total_blocks = CBD * lax.axis_size("ra")
    taper = taper_table(TILE)
    cosine, sine = fourier_tables(TILE)
    section_one = jnp.concatenate([cosine, sine], axis=1)
    section_two = jnp.concatenate([cosine, sine], axis=0)
    zero_index = jnp.zeros((), jnp.int32)

    def one_split(stokes_maps):
        flat = stokes_maps.reshape(STOKES * TILE, TILE)
        halfway = jnp.dot(flat, section_one, preferred_element_type=jnp.float32).astype(
            jnp.bfloat16
        )
        halfway = halfway.reshape(STOKES, TILE, 2 * TILE)
        outer = jnp.einsum("ky,mya->mka", section_two, halfway, preferred_element_type=jnp.float32)
        real_part = (outer[:, :TILE, :TILE] - outer[:, TILE:, TILE:]).astype(jnp.bfloat16)
        imag_part = (outer[:, :TILE, TILE:] + outer[:, TILE:, :TILE]).astype(jnp.bfloat16)
        return (real_part, imag_part)

    def one_tile(corner):
        local_column = (corner[1] - first_block) % total_blocks * BPX
        row_start = corner[0] * BPX
        tile_pixels = lax.dynamic_slice(
            window, (zero_index, zero_index, row_start, local_column), (SPLITS, STOKES, TILE, TILE)
        )
        values = tile_pixels.astype(jnp.float32)
        difference = values - jnp.mean(values, axis=0, keepdims=True)
        tapered = (difference * taper).astype(jnp.bfloat16)
        real_part, imag_part = lax.map(one_split, tapered)
        spectra = jnp.concatenate(
            [
                real_part.reshape(SPLITS * STOKES, TILE, TILE),
                imag_part.reshape(SPLITS * STOKES, TILE, TILE),
            ],
            axis=0,
        )
        return blockify(spectra)

    spectra_blocks = lax.map(one_tile, tile_start)
    owned = spectra_blocks.shape[0]
    local_cross = cross_power(spectra_blocks.reshape(owned, FBLK, 2, SPLITS, STOKES, FBS * FBS))
    cross = lax.all_to_all(local_cross, "ra", split_axis=1, concat_axis=0, tiled=True)
    block_mean = jnp.mean(cross, axis=-1, keepdims=True)
    level = jnp.mean(block_mean, axis=0, keepdims=True)
    kept = jnp.where((pattern == 1)[:, :, None, None], cross, block_mean)
    return 0.5 * kept + 0.5 * level


def combine(maps_ref, first_row, weight_y, weight_x, store):
    first = jnp.broadcast_to(first_row, (BPX, HALF))
    for block in range(TILE // BPX):
        place = (block - first) & 3
        up = jnp.where(place == 3, weight_y[1], 1.0)
        weight = jnp.where(place == 0, weight_y[0], up) * (0.5 * weight_x)
        upper = first <= block
        for p in range(STOKES):
            s = []
            for split in range(SPLITS):
                high = maps_ref[split, p, block * BPX : (block + 1) * BPX, :].astype(jnp.float32)
                low = maps_ref[
                    split, p, TILE + block * BPX : TILE + (block + 1) * BPX, :
                ].astype(jnp.float32)
                s.append(jnp.where(upper, high, low))
            sum_a, sum_b = s[0] + s[1], s[2] + s[3]
            dif_a, dif_b = s[0] - s[1], s[2] - s[3]
            for k, value in enumerate((sum_a - sum_b, dif_a + dif_b, dif_a - dif_b)):
                store(k, p * TILE + block * BPX, (value * weight).astype(jnp.bfloat16))


def pick_x(offset_row, wx_ref, lanes):
    rows = [wx_ref[m : m + 1, lanes] for m in range(3)]
    return jnp.where(offset_row == 0, rows[0], jnp.where(offset_row == 1, rows[1], rows[2]))


def power_kernel(
    n,
    info_ref,
    maps_ref,
    wy_ref,
    wx_ref,
    t1_ref,
    t2_ref,
    out_ref,
    info_in,
    halo_out,
    halo_in,
    own,
    half_ref,
    spec,
    cross,
    shuffle,
    packed,
    info_send,
    info_recv,
    halo_send,
    halo_recv,
    all_send,
    all_recv,
    local_sem,
):
    me = lax.axis_index("ra")
    right, left = lax.rem(me + 1, n), lax.rem(me + n - 1, n)

    barrier = pltpu.get_barrier_semaphore()

    @pl.loop(1, n)
    def _(step):
        pl.semaphore_signal(
            barrier, inc=1, device_id={"ra": lax.rem(me + step, n)}, device_id_type=MESH
        )

    pl.semaphore_wait(barrier, n - 1)

    def info_copy(side):
        return pltpu.make_async_remote_copy(
            src_ref=info_ref,
            dst_ref=info_in.at[side],
            send_sem=info_send.at[side],
            recv_sem=info_recv.at[side],
            device_id={"ra": (right, left)[side]},
            device_id_type=MESH,
        )

    def halo_copy(side, k):
        return pltpu.make_async_remote_copy(
            src_ref=halo_out.at[side, k],
            dst_ref=halo_in.at[side, k],
            send_sem=halo_send.at[side, k],
            recv_sem=halo_recv.at[side, k],
            device_id={"ra": (right, left)[side]},
            device_id_type=MESH,
        )

    def power_copy(to, source):
        return pltpu.make_async_remote_copy(
            src_ref=packed.at[to],
            dst_ref=out_ref.at[source],
            send_sem=all_send.at[to],
            recv_sem=all_recv.at[source],
            device_id={"ra": to},
            device_id_type=MESH,
        )

    for side in range(2):
        info_copy(side).start()

    lane = lax.broadcasted_iota(jnp.int32, (1, HALF), 1)

    def store_own(k, row, value):
        own[k, row : row + BPX, :] = value

    combine(
        maps_ref,
        info_ref[0:1, :],
        wy_ref,
        pick_x(info_ref[1:2, :], wx_ref, slice(HALF, TILE)),
        store_own,
    )

    for side in range(2):
        info_copy(1 - side).wait_recv()
        offset_row = info_in[1 - side, 1:2, :]
        weight_x = pick_x(offset_row, wx_ref, slice(0, HALF))
        inside = (lane >= BPX * offset_row) if side == 0 else (lane < BPX * offset_row)

        def store_halo(k, row, value):
            halo_out[side, k, row : row + BPX, :] = value

        combine(
            maps_ref,
            info_in[1 - side, 0:1, :],
            wy_ref,
            jnp.where(inside, weight_x, 0.0),
            store_halo,
        )
        for k in range(COMBOS):
            halo_copy(side, k).start()

    cross[...] = jnp.zeros_like(cross)

    @pl.loop(0, COMBOS)
    def _(k):
        for side in range(2):
            halo_copy(side, k).wait_recv()
        for p in range(STOKES):
            rows = slice(p * TILE, (p + 1) * TILE)
            outer = halo_in[0, k, rows, :] + halo_in[1, k, rows, :]
            pixels = jnp.concatenate([outer, own[k, rows, :]], axis=1)
            half_ref[0:TILE, :] = jnp.dot(
                pixels, t1_ref[:, 0:TILE], preferred_element_type=jnp.float32
            ).astype(jnp.bfloat16)
            half_ref[TILE : 2 * TILE, :] = jnp.dot(
                pixels, t1_ref[:, TILE : 2 * TILE], preferred_element_type=jnp.float32
            ).astype(jnp.bfloat16)
            spec[p] = jnp.dot(t2_ref[...], half_ref[...], preferred_element_type=jnp.float32)

        @pl.loop(0, TILE // 16)
        def _(step):
            start = pl.multiple_of(step * 16, 16)
            real = [spec[p, pl.ds(start, 16), :] for p in range(STOKES)]
            imag = [spec[p, pl.ds(start + TILE, 16), :] for p in range(STOKES)]
            for c, (a, b) in enumerate(cov_pairs):
                cross[c, pl.ds(start, 16), :] += real[a] * real[b] + imag[a] * imag[b]

    my_half = me // 8

    @pl.loop(0, 2)
    def _(turn):
        part = lax.rem(my_half + 1 + turn, 2)
        base = part * HALF

        @pl.loop(0, PAIRS)
        def _(c):
            for ih in range(2):
                for vh in range(2):
                    x = [
                        cross[
                            c,
                            pl.ds(pl.multiple_of(base + (8 * ih + i) * 8, 8), 8),
                            vh * HALF : (vh + 1) * HALF,
                        ]
                        for i in range(8)
                    ]
                    for bit in range(3):
                        shift = FBS << bit
                        low = ((lane >> (4 + bit)) & 1) == 0
                        y = list(x)
                        for i in range(8):
                            if not i >> bit & 1:
                                j = i | 1 << bit
                                y[i] = jnp.where(low, x[i], pltpu.roll(x[j], shift, 1))
                                y[j] = jnp.where(low, pltpu.roll(x[i], HALF - shift, 1), x[j])
                        x = y
                    for v in range(8):
                        shuffle[ih, pl.ds((8 * vh + v) * PAIRS + c, 8, stride=FBN * PAIRS), :] = x[v]

        @pl.loop(0, 8)
        def _(step):
            u = lax.rem(me + step, 8)
            to = part * 8 + u
            rows = pl.ds(pl.multiple_of(u * FBN * PAIRS, 8), FBN * PAIRS)
            for ih in range(2):
                packed[to, :, ih * HALF : (ih + 1) * HALF] = (
                    shuffle[ih, rows, :] * 0.25
                ).astype(jnp.bfloat16)

            @pl.when(to != me)
            def _():
                power_copy(to, me).start()

            @pl.when(to == me)
            def _():
                pltpu.make_async_copy(packed.at[me], out_ref.at[me], local_sem).start()

    for side in range(2):
        info_copy(side).wait_send()
        for k in range(COMBOS):
            halo_copy(side, k).wait_send()
    pltpu.make_async_copy(packed.at[me], out_ref.at[me], local_sem).wait()

    @pl.loop(1, n)
    def _(step):
        other = lax.rem(me + step, n)
        power_copy(other, other).wait_recv()
        power_copy(other, other).wait_send()


def finish_kernel(pattern_ref, ones_ref, power_ref, out_ref, wide, means):
    tiles, rows = power_ref.shape[0], power_ref.shape[1]
    level = jnp.zeros((rows, HALF), jnp.float32)
    for t in range(tiles):
        values = power_ref[t]
        mean = jnp.dot(values, ones_ref[...], preferred_element_type=jnp.float32)
        means[t] = mean
        level = level + mean
        wide[t] = values.astype(jnp.float32)
    means[tiles] = level * (0.5 / tiles)
    blocks = rows // PAIRS

    @pl.loop(0, tiles)
    def _(t):
        for v in range(blocks):
            own = slice(v * PAIRS, (v + 1) * PAIRS)
            keep = pattern_ref[t, v] == 1
            mean, base = means[t, own, :], means[tiles, own, :]
            for ih in range(2):
                lanes = slice(ih * HALF, (ih + 1) * HALF)
                kept = jnp.where(keep, wide[t, own, lanes], mean)
                out_ref[t, v, :, lanes] = 0.5 * kept + base


def kernel_body(split_maps, tile_start, pattern):
    n = lax.axis_size("ra")
    offset = (tile_start[0, 1] - (lax.axis_index("ra") - REACH) * CBD) % (CBD * n)
    row = lax.broadcasted_iota(jnp.int32, (8, HALF), 0)
    info = jnp.where(row == 0, tile_start[0, 0], offset).astype(jnp.int32)
    cosine, sine = fourier_tables(TILE)
    section_one = jnp.concatenate([cosine, sine], axis=1)
    order = jnp.asarray(
        [16 * (8 * h + u) + i for h in range(2) for i in range(16) for u in range(8)], jnp.int32
    )
    order_cos, order_sin = cosine[order], sine[order]
    section_two = jnp.concatenate(
        [
            jnp.concatenate([order_cos, -order_sin], axis=1),
            jnp.concatenate([order_sin, order_cos], axis=1),
        ],
        axis=0,
    )
    edge = TILE // 8
    counter = jnp.arange(TILE, dtype=jnp.float32)
    rising = jnp.where(counter < edge, jnp.sin(math.pi * (counter + 0.5) / (2 * edge)) ** 2, 1.0)
    line = rising * rising[::-1]
    weight_y = jnp.broadcast_to(
        jnp.stack([line[:BPX], line[TILE - BPX :]])[:, :, None], (2, BPX, HALF)
    )
    weight_x = jnp.stack([jnp.roll(line, BPX * (m % 4)) for m in range(8)])
    rows = FBN * PAIRS
    vmem = pl.BlockSpec(memory_space=pltpu.VMEM)
    power = pl.pallas_call(
        functools.partial(power_kernel, n),
        out_shape=jax.ShapeDtypeStruct((n, rows, TILE), jnp.bfloat16),
        in_specs=[vmem] * 6,
        out_specs=pl.BlockSpec(memory_space=pl.ANY),
        scratch_shapes=[
            pltpu.VMEM((2, 8, HALF), jnp.int32),
            pltpu.VMEM((2, COMBOS, STOKES * TILE, HALF), jnp.bfloat16),
            pltpu.VMEM((2, COMBOS, STOKES * TILE, HALF), jnp.bfloat16),
            pltpu.VMEM((COMBOS, STOKES * TILE, HALF), jnp.bfloat16),
            pltpu.VMEM((2 * TILE, TILE), jnp.bfloat16),
            pltpu.VMEM((STOKES, 2 * TILE, TILE), jnp.float32),
            pltpu.VMEM((PAIRS, TILE, TILE), jnp.float32),
            pltpu.VMEM((2, 8 * rows, HALF), jnp.float32),
            pltpu.VMEM((n, rows, TILE), jnp.bfloat16),
            pltpu.SemaphoreType.DMA((2,)),
            pltpu.SemaphoreType.DMA((2,)),
            pltpu.SemaphoreType.DMA((2, COMBOS)),
            pltpu.SemaphoreType.DMA((2, COMBOS)),
            pltpu.SemaphoreType.DMA((n,)),
            pltpu.SemaphoreType.DMA((n,)),
            pltpu.SemaphoreType.DMA,
        ],
        compiler_params=pltpu.CompilerParams(
            collective_id=0, has_side_effects=True, vmem_limit_bytes=48 * 2**20
        ),
    )(info, split_maps, weight_y, weight_x, section_one, section_two)
    ones = jnp.full((TILE, HALF), 1.0 / TILE, jnp.bfloat16)
    return pl.pallas_call(
        finish_kernel,
        out_shape=jax.ShapeDtypeStruct((n, FBN, PAIRS, TILE), jnp.float32),
        in_specs=[pl.BlockSpec(memory_space=pltpu.SMEM), vmem, vmem],
        out_specs=vmem,
        scratch_shapes=[
            pltpu.VMEM((n, rows, TILE), jnp.float32),
            pltpu.VMEM((n + 1, rows, HALF), jnp.float32),
        ],
        compiler_params=pltpu.CompilerParams(vmem_limit_bytes=32 * 2**20),
    )(pattern, ones, power)


def body(split_maps, tile_start, pattern):
    if lax.axis_size("ra") == FBN:
        return kernel_body(split_maps, tile_start, pattern)
    return plain_body(split_maps, tile_start, pattern)


def solution(mesh):
    placed = (P(None, None, "grp", "ra"), P(("grp", "ra"), None), P("grp", "ra"))
    return jax.shard_map(
        body, mesh=mesh, in_specs=placed, out_specs=P("grp", "ra", None, None), check_vma=False
    )
```

```python
import functools
import math

import jax
import jax.numpy as jnp
import ml_dtypes
import numpy as np
from jax import lax
from jax.experimental import pallas as pl
from jax.experimental.pallas import tpu as pltpu
from jax.sharding import PartitionSpec as P

SPLITS = 4
STOKES = 3
BPX = 64
CBD = 2
REACH = 1
FBN = 16
TILE = 256
FBS = 16
FBLK = 256
PAIRS = 6
COMBOS = 3
HALF = 128
MESH = pl.DeviceIdType.MESH


cov_pairs = ((0, 0), (1, 1), (2, 2), (0, 1), (0, 2), (1, 2))


def with_halo(shard, sides, width):
    for axis, dim in sides:
        size, length = (lax.axis_size(axis), shard.shape[dim])
        up = [(i, (i + 1) % size) for i in range(size)]
        down = [(j, i) for i, j in up]
        last = lax.slice_in_dim(shard, length - width, length, axis=dim)
        initial = lax.slice_in_dim(shard, 0, width, axis=dim)
        before = lax.ppermute(last, axis, up)
        after = lax.ppermute(initial, axis, down)
        shard = jnp.concatenate([before, shard, after], axis=dim)
    return shard


def fourier_tables(length):
    counter = jnp.arange(length, dtype=jnp.int32)
    phase = counter[:, None] * counter[None, :] % length
    angle = 2.0 * math.pi / length * phase.astype(jnp.float32)
    factor = 1.0 / math.sqrt(length)
    return (
        (jnp.cos(angle) * factor).astype(jnp.bfloat16),
        (jnp.sin(angle) * factor).astype(jnp.bfloat16),
    )


def taper_table(length):
    edge = length // 8
    counter = jnp.arange(length, dtype=jnp.float32)
    rising = jnp.where(counter < edge, jnp.sin(math.pi * (counter + 0.5) / (2 * edge)) ** 2, 1.0)
    line = rising * rising[::-1]
    return line[:, None] * line[None, :]


def blockify(spectra):
    count = spectra.shape[0]
    shaped = spectra.reshape(count, FBN, FBS, FBN, FBS)
    return shaped.transpose(1, 3, 0, 2, 4).reshape(FBN * FBN, count, FBS * FBS)


def cross_power(stacked):
    values = stacked.astype(jnp.float32)
    real_part = values[..., 0, :, :, :]
    imag_part = values[..., 1, :, :, :]
    terms = []
    for first_axis, second_axis in cov_pairs:
        product = (
            real_part[..., first_axis, :] * real_part[..., second_axis, :]
            + imag_part[..., first_axis, :] * imag_part[..., second_axis, :]
        )
        terms.append(jnp.mean(product, axis=-2))
    return jnp.stack(terms, axis=-2)


def plain_body(split_maps, tile_start, pattern):
    width = REACH * CBD * BPX
    window = with_halo(split_maps, (("ra", 3),), width)
    first_block = (lax.axis_index("ra") - REACH) * CBD
    total_blocks = CBD * lax.axis_size("ra")
    taper = taper_table(TILE)
    cosine, sine = fourier_tables(TILE)
    section_one = jnp.concatenate([cosine, sine], axis=1)
    section_two = jnp.concatenate([cosine, sine], axis=0)
    zero_index = jnp.zeros((), jnp.int32)

    def one_split(stokes_maps):
        flat = stokes_maps.reshape(STOKES * TILE, TILE)
        halfway = jnp.dot(flat, section_one, preferred_element_type=jnp.float32).astype(
            jnp.bfloat16
        )
        halfway = halfway.reshape(STOKES, TILE, 2 * TILE)
        outer = jnp.einsum("ky,mya->mka", section_two, halfway, preferred_element_type=jnp.float32)
        real_part = (outer[:, :TILE, :TILE] - outer[:, TILE:, TILE:]).astype(jnp.bfloat16)
        imag_part = (outer[:, :TILE, TILE:] + outer[:, TILE:, :TILE]).astype(jnp.bfloat16)
        return (real_part, imag_part)

    def one_tile(corner):
        local_column = (corner[1] - first_block) % total_blocks * BPX
        row_start = corner[0] * BPX
        tile_pixels = lax.dynamic_slice(
            window, (zero_index, zero_index, row_start, local_column), (SPLITS, STOKES, TILE, TILE)
        )
        values = tile_pixels.astype(jnp.float32)
        difference = values - jnp.mean(values, axis=0, keepdims=True)
        tapered = (difference * taper).astype(jnp.bfloat16)
        real_part, imag_part = lax.map(one_split, tapered)
        spectra = jnp.concatenate(
            [
                real_part.reshape(SPLITS * STOKES, TILE, TILE),
                imag_part.reshape(SPLITS * STOKES, TILE, TILE),
            ],
            axis=0,
        )
        return blockify(spectra)

    spectra_blocks = lax.map(one_tile, tile_start)
    owned = spectra_blocks.shape[0]
    local_cross = cross_power(spectra_blocks.reshape(owned, FBLK, 2, SPLITS, STOKES, FBS * FBS))
    cross = lax.all_to_all(local_cross, "ra", split_axis=1, concat_axis=0, tiled=True)
    block_mean = jnp.mean(cross, axis=-1, keepdims=True)
    level = jnp.mean(block_mean, axis=0, keepdims=True)
    kept = jnp.where((pattern == 1)[:, :, None, None], cross, block_mean)
    return 0.5 * kept + 0.5 * level


arrival_pairs = ((0, 0), (1, 1), (0, 1), (2, 2), (0, 2), (1, 2))
places = tuple(cov_pairs.index(pair) for pair in arrival_pairs)
pieces = ((0, 1), (1, 2), (3, 3))


def combine(maps_ref, p, first_row, weight_y, weight_x, target):
    first = jnp.broadcast_to(first_row, (BPX, HALF))
    for block in range(TILE // BPX):
        place = (block - first) & 3
        up = jnp.where(place == 3, weight_y[1], 1.0)
        weight = jnp.where(place == 0, weight_y[0], up) * (0.5 * weight_x)
        upper = first <= block
        s = []
        for split in range(SPLITS):
            high = maps_ref[split, p, block * BPX : (block + 1) * BPX, :].astype(jnp.float32)
            low = maps_ref[
                split, p, TILE + block * BPX : TILE + (block + 1) * BPX, :
            ].astype(jnp.float32)
            s.append(jnp.where(upper, high, low))
        sum_a, sum_b = s[0] + s[1], s[2] + s[3]
        dif_a, dif_b = s[0] - s[1], s[2] - s[3]
        for k, value in enumerate((sum_a - sum_b, dif_a + dif_b, dif_a - dif_b)):
            row = k * TILE + block * BPX
            target[row : row + BPX, :] = (value * weight).astype(jnp.bfloat16)


def pick_x(offset_row, wx_ref, lanes):
    rows = [wx_ref[m : m + 1, lanes] for m in range(3)]
    return jnp.where(offset_row == 0, rows[0], jnp.where(offset_row == 1, rows[1], rows[2]))


def power_kernel(
    n,
    corner_ref,
    maps_in,
    wy_in,
    wx_in,
    t1_in,
    t2_in,
    out_ref,
    maps_ref,
    wy_ref,
    wx_ref,
    t1_ref,
    t2_ref,
    info_ref,
    info_in,
    halo_out,
    halo_in,
    own,
    half_ref,
    spec,
    cross,
    shuffle,
    packed,
    info_send,
    info_recv,
    halo_send,
    halo_recv,
    all_send,
    all_recv,
    local_sem,
    load_sem,
):
    me = lax.axis_index("ra")
    right, left = lax.rem(me + 1, n), lax.rem(me + n - 1, n)

    loads = [
        pltpu.make_async_copy(source, target, load_sem.at[i])
        for i, (source, target) in enumerate(
            (
                (maps_in, maps_ref),
                (wy_in, wy_ref),
                (wx_in, wx_ref),
                (t1_in, t1_ref),
                (t2_in, t2_ref),
            )
        )
    ]
    for load in loads:
        load.start()
    row = lax.broadcasted_iota(jnp.int32, (8, HALF), 0)
    offset = lax.rem(corner_ref[0, 1] - (me - REACH) * CBD + CBD * n, CBD * n)
    info_ref[...] = jnp.where(row == 0, corner_ref[0, 0], offset)

    barrier = pltpu.get_barrier_semaphore()

    @pl.loop(1, n)
    def _(step):
        pl.semaphore_signal(
            barrier, inc=1, device_id={"ra": lax.rem(me + step, n)}, device_id_type=MESH
        )

    pl.semaphore_wait(barrier, n - 1)

    def info_copy(side):
        return pltpu.make_async_remote_copy(
            src_ref=info_ref,
            dst_ref=info_in.at[side],
            send_sem=info_send.at[side],
            recv_sem=info_recv.at[side],
            device_id={"ra": (right, left)[side]},
            device_id_type=MESH,
        )

    def halo_copy(side, p):
        return pltpu.make_async_remote_copy(
            src_ref=halo_out.at[side, p],
            dst_ref=halo_in.at[side, p],
            send_sem=halo_send.at[side, p],
            recv_sem=halo_recv.at[side, p],
            device_id={"ra": (right, left)[side]},
            device_id_type=MESH,
        )

    def power_copy(piece, to, source):
        first, count = pieces[piece]
        rows = pl.ds(first * FBN, count * FBN)
        return pltpu.make_async_remote_copy(
            src_ref=packed.at[to, rows],
            dst_ref=out_ref.at[source, rows],
            send_sem=all_send.at[piece, to],
            recv_sem=all_recv.at[piece, source],
            device_id={"ra": to},
            device_id_type=MESH,
        )

    for side in range(2):
        info_copy(side).start()

    lane = lax.broadcasted_iota(jnp.int32, (1, HALF), 1)
    for load in loads[:3]:
        load.wait()

    own_x = pick_x(info_ref[1:2, :], wx_ref, slice(HALF, TILE))
    for p in range(STOKES):
        combine(maps_ref, p, info_ref[0:1, :], wy_ref, own_x, own.at[p])

    halo_x = []
    for side in range(2):
        info_copy(1 - side).wait_recv()
        offset_row = info_in[1 - side, 1:2, :]
        inside = (lane >= BPX * offset_row) if side == 0 else (lane < BPX * offset_row)
        halo_x.append(jnp.where(inside, pick_x(offset_row, wx_ref, slice(0, HALF)), 0.0))
    for p in range(STOKES):
        for side in range(2):
            combine(
                maps_ref,
                p,
                info_in[1 - side, 0:1, :],
                wy_ref,
                halo_x[side],
                halo_out.at[side, p],
            )
            halo_copy(side, p).start()
    for load in loads[3:]:
        load.wait()

    my_half = me // 8
    for p in range(STOKES):
        for side in range(2):
            halo_copy(side, p).wait_recv()

        @pl.loop(0, COMBOS)
        def _(k):
            rows = pl.ds(pl.multiple_of(k * TILE, TILE), TILE)
            outer = halo_in[0, p, rows, :] + halo_in[1, p, rows, :]
            pixels = jnp.concatenate([outer, own[p, rows, :]], axis=1)
            half_ref[0:TILE, :] = jnp.dot(
                pixels, t1_ref[:, 0:TILE], preferred_element_type=jnp.float32
            ).astype(jnp.bfloat16)
            half_ref[TILE : 2 * TILE, :] = jnp.dot(
                pixels, t1_ref[:, TILE : 2 * TILE], preferred_element_type=jnp.float32
            ).astype(jnp.bfloat16)
            spec[p, k] = jnp.dot(t2_ref[...], half_ref[...], preferred_element_type=jnp.float32)

        first, count = pieces[p]

        @pl.loop(0, TILE // 8)
        def _(step):
            start = pl.multiple_of(step * 8, 8)
            total = [None] * count
            for k in range(COMBOS):
                real = [spec[q, k, pl.ds(start, 8), :] for q in range(p + 1)]
                imag = [spec[q, k, pl.ds(start + TILE, 8), :] for q in range(p + 1)]
                for i, (a, b) in enumerate(arrival_pairs[first : first + count]):
                    term = real[a] * real[b] + imag[a] * imag[b]
                    total[i] = term if k == 0 else total[i] + term
            for i in range(count):
                cross[first + i, pl.ds(start, 8), :] = 0.25 * total[i]

        @pl.loop(0, 2)
        def _(turn):
            part = lax.rem(my_half + 1 + turn, 2)
            base = part * HALF

            @pl.loop(first, first + count)
            def _(c):
                for ih in range(2):
                    for vh in range(2):
                        x = [
                            cross[
                                c,
                                pl.ds(pl.multiple_of(base + (8 * ih + i) * 8, 8), 8),
                                vh * HALF : (vh + 1) * HALF,
                            ]
                            for i in range(8)
                        ]
                        for bit in range(3):
                            shift = FBS << bit
                            low = ((lane >> (4 + bit)) & 1) == 0
                            y = list(x)
                            for i in range(8):
                                if not i >> bit & 1:
                                    j = i | 1 << bit
                                    y[i] = jnp.where(low, x[i], pltpu.roll(x[j], shift, 1))
                                    y[j] = jnp.where(low, pltpu.roll(x[i], HALF - shift, 1), x[j])
                            x = y
                        for v in range(8):
                            rows = pl.ds(c * FBN + 8 * vh + v, 8, stride=FBN * PAIRS)
                            shuffle[ih, rows, :] = x[v]

            @pl.loop(0, 8)
            def _(step):
                u = lax.rem(me + step, 8)
                to = part * 8 + u
                rows = pl.ds(pl.multiple_of(u * FBN * PAIRS + first * FBN, 8), count * FBN)
                for ih in range(2):
                    packed[
                        to, first * FBN : (first + count) * FBN, ih * HALF : (ih + 1) * HALF
                    ] = shuffle[ih, rows, :].astype(jnp.bfloat16)

                @pl.when(to != me)
                def _():
                    power_copy(p, to, me).start()

    mine = pltpu.make_async_copy(packed.at[me], out_ref.at[me], local_sem)
    mine.start()
    for side in range(2):
        info_copy(side).wait_send()
        for p in range(STOKES):
            halo_copy(side, p).wait_send()

    for p in range(STOKES):

        @pl.loop(1, n)
        def _(step):
            other = lax.rem(me + step, n)
            power_copy(p, other, other).wait_recv()
            power_copy(p, other, other).wait_send()

    mine.wait()


def finish_kernel(pattern_in, power_in, out_ref, pattern_ref, power_ref, means, load_sem):
    tiles, rows = power_ref.shape[:2]
    step, count = pl.program_id(0), out_ref.shape[0]

    @pl.when(step == 0)
    def _():
        loads = [
            pltpu.make_async_copy(power_in, power_ref, load_sem.at[0]),
            pltpu.make_async_copy(pattern_in, pattern_ref, load_sem.at[1]),
        ]
        for load in loads:
            load.start()
        for load in loads:
            load.wait()
        ones = jnp.full((TILE, HALF), 1.0 / TILE, jnp.bfloat16)
        level = jnp.zeros((rows, HALF), jnp.float32)
        for t in range(tiles):
            mean = jnp.dot(power_ref[t], ones, preferred_element_type=jnp.float32)
            means[t] = mean
            level = level + mean
        means[tiles] = level * (0.5 / tiles)

    square = (FBN, FBN)
    diagonal = lax.broadcasted_iota(jnp.int32, square, 0) == lax.broadcasted_iota(
        jnp.int32, square, 1
    )
    for i in range(count):
        t = step * count + i
        chosen = jnp.where(diagonal & (pattern_ref[pl.ds(t, 1), :] == 1), 1.0, 0.0)
        keep = jnp.broadcast_to(jnp.sum(chosen, axis=1, keepdims=True), (FBN, HALF)) > 0.5
        for c in range(PAIRS):
            own = slice(c * FBN, (c + 1) * FBN)
            mean, base = means[t, own, :], means[tiles, own, :]
            for ih in range(2):
                lanes = slice(ih * HALF, (ih + 1) * HALF)
                kept = jnp.where(keep, power_ref[t, own, lanes].astype(jnp.float32), mean)
                out_ref[i, places[c], :, lanes] = 0.5 * kept + base


def constant_tables():
    counter = np.arange(TILE)
    angle = 2.0 * math.pi / TILE * (counter[:, None] * counter[None, :] % TILE)
    cosine, sine = np.cos(angle) / math.sqrt(TILE), np.sin(angle) / math.sqrt(TILE)
    section_one = np.concatenate([cosine, sine], axis=1)
    order = counter.reshape(2, 8, FBS).transpose(0, 2, 1).reshape(-1)
    cosine, sine = cosine[order], sine[order]
    section_two = np.block([[cosine, -sine], [sine, cosine]])
    edge = TILE // 8
    rising = np.where(counter < edge, np.sin(math.pi * (counter + 0.5) / (2 * edge)) ** 2, 1.0)
    line = (rising * rising[::-1]).astype(np.float32)
    weight_y = np.stack([line[:BPX], line[TILE - BPX :]])
    weight_y = np.ascontiguousarray(np.broadcast_to(weight_y[:, :, None], (2, BPX, HALF)))
    weight_x = np.stack([np.roll(line, BPX * (m % 4)) for m in range(8)])
    low = ml_dtypes.bfloat16
    single = lambda table: table.astype(np.float32).astype(low)
    return weight_y, weight_x, single(section_one), single(section_two)


def kernel_body(split_maps, tile_start, pattern):
    n = lax.axis_size("ra")
    weight_y, weight_x, section_one, section_two = map(jnp.asarray, constant_tables())
    rows = FBN * PAIRS
    smem = pl.BlockSpec(memory_space=pltpu.SMEM)
    hbm = pl.BlockSpec(memory_space=pltpu.HBM)
    power = pl.pallas_call(
        functools.partial(power_kernel, n),
        out_shape=jax.ShapeDtypeStruct((n, rows, TILE), jnp.bfloat16),
        in_specs=[smem] + [hbm] * 5,
        out_specs=pl.BlockSpec(memory_space=pl.ANY),
        scratch_shapes=[
            pltpu.VMEM(split_maps.shape, jnp.bfloat16),
            pltpu.VMEM(weight_y.shape, jnp.float32),
            pltpu.VMEM(weight_x.shape, jnp.float32),
            pltpu.VMEM(section_one.shape, jnp.bfloat16),
            pltpu.VMEM(section_two.shape, jnp.bfloat16),
            pltpu.VMEM((8, HALF), jnp.int32),
            pltpu.VMEM((2, 8, HALF), jnp.int32),
            pltpu.VMEM((2, STOKES, COMBOS * TILE, HALF), jnp.bfloat16),
            pltpu.VMEM((2, STOKES, COMBOS * TILE, HALF), jnp.bfloat16),
            pltpu.VMEM((STOKES, COMBOS * TILE, HALF), jnp.bfloat16),
            pltpu.VMEM((2 * TILE, TILE), jnp.bfloat16),
            pltpu.VMEM((STOKES, COMBOS, 2 * TILE, TILE), jnp.float32),
            pltpu.VMEM((PAIRS, TILE, TILE), jnp.float32),
            pltpu.VMEM((2, 8 * rows, HALF), jnp.float32),
            pltpu.VMEM((n, rows, TILE), jnp.bfloat16),
            pltpu.SemaphoreType.DMA((2,)),
            pltpu.SemaphoreType.DMA((2,)),
            pltpu.SemaphoreType.DMA((2, STOKES)),
            pltpu.SemaphoreType.DMA((2, STOKES)),
            pltpu.SemaphoreType.DMA((len(pieces), n)),
            pltpu.SemaphoreType.DMA((len(pieces), n)),
            pltpu.SemaphoreType.DMA,
            pltpu.SemaphoreType.DMA((5,)),
        ],
        compiler_params=pltpu.CompilerParams(
            collective_id=0, has_side_effects=True, vmem_limit_bytes=64 * 2**20 - 2**16
        ),
    )(tile_start, split_maps, weight_y, weight_x, section_one, section_two)
    count = n // 4
    result = pl.pallas_call(
        finish_kernel,
        out_shape=jax.ShapeDtypeStruct((n, PAIRS, FBN, TILE), jnp.float32),
        grid=(n // count,),
        in_specs=[hbm, hbm],
        out_specs=pl.BlockSpec((count, PAIRS, FBN, TILE), lambda step: (step, 0, 0, 0)),
        scratch_shapes=[
            pltpu.VMEM(pattern.shape, jnp.int32),
            pltpu.VMEM(power.shape, jnp.bfloat16),
            pltpu.VMEM((n + 1, rows, HALF), jnp.float32),
            pltpu.SemaphoreType.DMA((2,)),
        ],
        compiler_params=pltpu.CompilerParams(vmem_limit_bytes=64 * 2**20 - 2**16),
    )(pattern, power)
    return result.transpose(0, 2, 1, 3)


def body(split_maps, tile_start, pattern):
    if lax.axis_size("ra") == FBN:
        return kernel_body(split_maps, tile_start, pattern)
    return plain_body(split_maps, tile_start, pattern)


def solution(mesh):
    placed = (P(None, None, "grp", "ra"), P(("grp", "ra"), None), P("grp", "ra"))
    return jax.shard_map(
        body, mesh=mesh, in_specs=placed, out_specs=P("grp", "ra", None, None), check_vma=False
    )
```
